32 devices in a mesh: row: 4 (over y, x), col: 8 (over z, core).
Axes of the slice: x: 2, y: 2, z: 4, core: 2. Of those that a mesh axis runs over, the one named last changes fastest.
Arguments:
- state: float32 [6, 137, 128, 512], P(None, None, 'col', 'row'), may hold values from -2 to 2, as said below
- conv_mask: int32 [128, 512], P('col', 'row'), may hold values from 0 to 1, as said below
- micro_mask: int32 [128, 512], P('col', 'row'), may hold values from 0 to 1, as said below
- w_in: bfloat16 [1024, 822], replicated, may hold values from -0.21875 to 0.21875
- w_hidden: bfloat16 [2, 1024, 1024], replicated, may hold values from -0.1875 to 0.1875
- w_out: bfloat16 [548, 1024], replicated, may hold values from -0.03125 to 0.03125
Outputs:
- advanced: float32 [6, 137, 128, 512], P(None, None, 'col', 'row')
- tendency: float32 [6, 137, 128, 512], P(None, None, 'col', 'row')
The draws below stay inside these ranges and needn't reach their ends.
Inputs may be any that keep to these rules, and one draw needn't show every extreme that they name: `state`: temperature, vapour, cloud water and rain lie in 0.2 to 2, the two winds in -2 to 2. `conv_mask`: 1 marks an active column; activity is clustered in tiles of 16 x 128 columns. `micro_mask`: 1 marks an active column; activity is clustered in tiles of 16 x 128 columns.
All inputs are finite; a program needn't handle non-finite values.
Results may differ from the reference program's by a relative error of at most 0.00053.
Values sent between devices are 32-bit elements; how exact they have to be, the bound alone decides.
A program may use at most 192 MiB of HBM per device.

```python
import jax
import jax.numpy as jnp
from jax import lax

LEV = 137
HID = 1024
CX = 16
CY = 128
ITERS = 3
NX = 128
NY = 512


def tiled_mask(key, light):
    first, second = jax.random.split(key)
    heavy = jax.random.randint(first, (NX // CX, NY // CY), 0, 4) == 0
    level = jnp.where(heavy, 16, light)
    level = jnp.repeat(jnp.repeat(level, CX, axis=0), CY, axis=1)
    pick = jax.random.randint(second, (NX, NY), 0, 16)
    return (pick < level).astype(jnp.int32)


def draw_state(key, part):
    key = jax.random.fold_in(key, 31)
    unit = jax.random.uniform(key, (6, LEV, NX, NY), jnp.float32)
    lower = jnp.array([0.2, 0.2, 0.2, 0.2, -2.0, -2.0], jnp.float32).reshape(6, 1, 1, 1)
    upper = jnp.array([2.0, 2.0, 2.0, 2.0, 2.0, 2.0], jnp.float32).reshape(6, 1, 1, 1)
    return lower + (upper - lower) * unit


def draw_conv_mask(key, part):
    key = jax.random.fold_in(key, 11)
    return tiled_mask(key, 3)


def draw_micro_mask(key, part):
    key = jax.random.fold_in(key, 23)
    return tiled_mask(key, 5)


def noise(key, extent, scale, most, dtype=jnp.bfloat16):
    result = jax.random.normal(key, extent, jnp.float32) * scale
    return jnp.minimum(jnp.maximum(result, -most), most).astype(dtype)


def setup_inputs(seed: int = 0) -> dict:
    keys = jax.random.split(jax.random.key(seed), 7)
    return {
        "state": draw_state(jax.random.fold_in(keys[6], 71), 0),
        "conv_mask": draw_conv_mask(jax.random.fold_in(keys[6], 71), 0),
        "micro_mask": draw_micro_mask(jax.random.fold_in(keys[6], 71), 0),
        "w_in": noise(keys[3], (HID, 6 * LEV), (6 * LEV) ** -0.5, 0.21875),
        "w_hidden": noise(keys[4], (2, HID, HID), HID ** -0.5, 0.1875),
        "w_out": noise(keys[5], (4 * LEV, HID), (32 * HID) ** -0.5, 0.03125),
    }


def column_tend(cols, conv, micro, w_in, w_hidden, w_out):
    fields, levels, count = cols.shape
    z = cols.reshape(fields * levels, count).astype(jnp.bfloat16)
    hidden = jax.nn.silu(jnp.dot(w_in, z, preferred_element_type=jnp.float32)).astype(jnp.bfloat16)
    hidden = jax.nn.silu(jnp.dot(w_hidden[0], hidden, preferred_element_type=jnp.float32)).astype(jnp.bfloat16)
    hidden = jax.nn.silu(jnp.dot(w_hidden[1], hidden, preferred_element_type=jnp.float32)).astype(jnp.bfloat16)
    network_out = jnp.dot(w_out, hidden, preferred_element_type=jnp.float32).reshape(4, levels, count)
    temp, vapour, water = cols[0], cols[1], cols[2]
    for step in range(ITERS):
        satur = 0.5 * jnp.exp(0.5 * temp)
        delta = jnp.maximum(0.5 * (vapour - satur), -water)
        temp = temp + 0.5 * delta
        vapour = vapour - delta
        water = water + delta
    autoconv = 0.6 * jnp.maximum(water - 0.8, 0.0)
    water = water - autoconv
    return jnp.stack([
        conv * network_out[0] + micro * (temp - cols[0]),
        conv * network_out[1] + micro * (vapour - cols[1]),
        micro * (water - cols[2]),
        micro * autoconv,
        conv * network_out[2],
        conv * network_out[3],
    ])


def advance(ext):
    def shifted(a, b):
        return ext[..., 2 + a:ext.shape[-2] - 2 + a, 2 + b:ext.shape[-1] - 2 + b]
    center = shifted(0, 0)
    along_x = (8.0 * (shifted(1, 0) - shifted(-1, 0)) - (shifted(2, 0) - shifted(-2, 0))) / 12.0
    along_y = (8.0 * (shifted(0, 1) - shifted(0, -1)) - (shifted(0, 2) - shifted(0, -2))) / 12.0
    hyper = (shifted(2, 0) + shifted(-2, 0) + shifted(0, 2) + shifted(0, -2)
             - 4.0 * (shifted(1, 0) + shifted(-1, 0) + shifted(0, 1) + shifted(0, -1)) + 12.0 * center)
    return center - 0.15 * (center[4] * along_x + center[5] * along_y) - 0.06 * hyper


def reference(state, conv_mask, micro_mask, w_in, w_hidden, w_out):
    fields, levels, lon_cells, lat_cells = state.shape
    block_cols = CX * CY
    nblocks = (lon_cells * lat_cells) // block_cols
    cols = state.reshape(fields, levels, nblocks, block_cols).transpose(2, 0, 1, 3)
    conv = conv_mask.astype(jnp.float32).reshape(nblocks, block_cols)
    micro = micro_mask.astype(jnp.float32).reshape(nblocks, block_cols)

    def one_block(items):
        return column_tend(items[0], items[1], items[2], w_in, w_hidden, w_out)

    tend_blocks = lax.map(one_block, (cols, conv, micro))
    tendency = tend_blocks.transpose(1, 2, 0, 3).reshape(fields, levels, lon_cells, lat_cells)
    fields_now = state + tendency
    for step in range(2):
        ext = jnp.pad(fields_now, ((0, 0), (0, 0), (2, 2), (0, 0)), mode="wrap")
        ext = jnp.pad(ext, ((0, 0), (0, 0), (0, 0), (2, 2)))
        fields_now = lax.map(advance, ext.transpose(1, 0, 2, 3)).transpose(1, 0, 2, 3)
    return fields_now, tendency
```

```python
import functools

import jax
import jax.numpy as jnp
from jax import lax
from jax.experimental import pallas as pl
from jax.experimental.pallas import tpu as pltpu
from jax.sharding import PartitionSpec as P

ITERS = 3
LANES = 128
HALO = 4
VMEM_LIMIT = 56 * 1024 * 1024


def silu(v):
    half = 0.5 * v
    return half + half * jnp.tanh(half)


def network(z, w_in, w_hidden, w_out, h_a, h_b, out):
    hid = w_in.shape[0]
    part = 256

    def layer(weight, source, target):
        for m in range(0, hid, part):
            acc = jnp.dot(weight(m), source, preferred_element_type=jnp.float32)
            target[m : m + part, :] = silu(acc).astype(jnp.bfloat16)

    layer(lambda m: w_in[m : m + part, :], z, h_a)
    layer(lambda m: w_hidden[0, m : m + part, :], h_a[...], h_b)
    layer(lambda m: w_hidden[1, m : m + part, :], h_b[...], h_a)
    out[: w_out.shape[0], :] = jnp.dot(w_out[...], h_a[...], preferred_element_type=jnp.float32)


def saturate(temp, vapour, water):
    temp0, vapour0, water0 = temp, vapour, water
    for _ in range(ITERS):
        satur = 0.5 * jnp.exp(0.5 * temp)
        delta = jnp.maximum(0.5 * (vapour - satur), -water)
        temp = temp + 0.5 * delta
        vapour = vapour - delta
        water = water + delta
    autoconv = 0.6 * jnp.maximum(water - 0.8, 0.0)
    water = water - autoconv
    return temp - temp0, vapour - vapour0, water - water0, autoconv


def physics_rows(rows, levels, lon, state, conv, micro, weights, scr, put):
    w_in, w_hidden, w_out = weights
    h_a, h_b, out = scr

    def field(f, l):
        return state[pl.ds(f * levels * lon + l, levels, stride=lon), :]

    z = jnp.concatenate(
        [state[pl.ds(l, 6 * levels, stride=lon), :].astype(jnp.bfloat16) for l in rows], axis=1
    )
    network(z, w_in, w_hidden, w_out, h_a, h_b, out)
    for k, l in enumerate(rows):
        c = conv[pl.ds(l, 1), :].astype(jnp.float32)
        m = micro[pl.ds(l, 1), :].astype(jnp.float32)
        cols = slice(k * LANES, (k + 1) * LANES)

        def net(f):
            return c * out[f * levels : (f + 1) * levels, cols]

        temp, vapour, water = field(0, l), field(1, l), field(2, l)
        d_t, d_q, d_w, auto = saturate(temp, vapour, water)
        t0 = net(0) + m * d_t
        put(k, 0, temp + t0, t0)
        t1 = net(1) + m * d_q
        put(k, 1, vapour + t1, t1)
        t2 = m * d_w
        put(k, 2, water + t2, t2)
        t3 = m * auto
        put(k, 3, field(3, l) + t3, t3)
        t4 = net(2)
        put(k, 4, field(4, l) + t4, t4)
        t5 = net(3)
        put(k, 5, field(5, l) + t5, t5)


def edge_kernel(levels, lon, state, conv, micro, w_in, w_hidden, w_out, lo, hi, tlo, thi, h_a, h_b, out):
    @pl.loop(0, HALO // 2)
    def _(i):
        rows = [2 * i, 2 * i + 1, lon - HALO + 2 * i, lon - HALO + 2 * i + 1]

        def put(k, f, upd, tend):
            u_ref, t_ref = (lo, tlo) if k < 2 else (hi, thi)
            u_ref[2 * i + k % 2, f, :levels, :] = upd
            t_ref[2 * i + k % 2, f, :levels, :] = tend

        physics_rows(rows, levels, lon, state, conv, micro, (w_in, w_hidden, w_out), (h_a, h_b, out), put)


def pack(tile, tiles, lane):
    acc = None
    for j in range(tiles):
        turned = pltpu.roll(tile(j), (8 * j + 4) % LANES, 1)
        acc = turned if acc is None else jnp.where(lane // 8 == j, turned, acc)
    return acc


def inner_kernel(
    levels, lon, groups, tiles, state, conv, micro, w_in, w_hidden, w_out, lo, hi, tlo, thi,
    mid, tend, packed, h_a, h_b, out,
):
    @pl.loop(0, (lon - 2 * HALO) // 4)
    def _(i):
        rows = [HALO + 4 * i + k for k in range(4)]

        def put(k, f, upd, tnd):
            mid[4 * i + k, f, :levels, :] = upd
            tend[pl.ds(f * levels * lon + rows[k], levels, stride=lon), :] = tnd

        physics_rows(rows, levels, lon, state, conv, micro, (w_in, w_hidden, w_out), (h_a, h_b, out), put)

    @pl.loop(0, HALO)
    def _(i):
        for f in range(6):
            tend[pl.ds(f * levels * lon + i, levels, stride=lon), :] = tlo[i, f, :levels, :]
            tend[pl.ds(f * levels * lon + lon - HALO + i, levels, stride=lon), :] = thi[i, f, :levels, :]

    lane = lax.broadcasted_iota(jnp.int32, (8, LANES), 1)
    for source, first, count in ((lo, 0, HALO), (mid, HALO, lon - 2 * HALO), (hi, lon - HALO, HALO)):

        @pl.loop(0, count)
        def _(i, source=source, first=first):
            for f in range(6):
                for g in range(groups):
                    packed[first + i, f, g] = pack(
                        lambda j: source[i, f, pl.ds((g * tiles + j) * 8, 8), :], tiles, lane
                    )


def stencil(center, xs, ys, u, v):
    xm2, xm1, xp1, xp2 = xs
    ym2, ym1, yp1, yp2 = ys
    along_x = 8.0 * (xp1 - xm1) - (xp2 - xm2)
    along_y = 8.0 * (yp1 - ym1) - (yp2 - ym2)
    one = (xp1 + xm1) + (yp1 + ym1)
    two = (xp2 + xm2) + (yp2 + ym2)
    return 0.28 * center + (u * along_x + v * along_y) + (0.24 * one - 0.06 * two)


def y_shifts(center, beyond, masks):
    low1, low2, high1, high2 = masks
    return (
        pltpu.roll(jnp.where(high2, beyond, center), 2, 1),
        pltpu.roll(jnp.where(high1, beyond, center), 1, 1),
        pltpu.roll(jnp.where(low1, beyond, center), LANES - 1, 1),
        pltpu.roll(jnp.where(low2, beyond, center), LANES - 2, 1),
    )


def advect_kernel(lon, tiles, left, lo, mid, hi, right, px, halo, inside, adv, px_l, px_r, s1_halo, s1):
    lane = lax.broadcasted_iota(jnp.int32, (8, LANES), 1)
    slot = lane % 8
    masks = (lane == 0, lane < 2, lane == LANES - 1, lane >= LANES - 2)
    slot_masks = (slot == 4, (slot == 4) | (slot == 5), slot == 3, (slot == 3) | (slot == 2))
    ext = lon + 2 * HALO
    scale = -0.15 / 12.0

    def place(r):
        for ref, first, count in (
            (left, 0, HALO),
            (lo, HALO, HALO),
            (mid, 2 * HALO, lon - 2 * HALO),
            (hi, lon, HALO),
            (right, lon + HALO, HALO),
        ):
            if r < first + count:
                return ref, r - first

    for ref, target, at in ((left, px_l, HALO - 2), (right, px_r, 0)):
        for i in range(2):

            @pl.loop(0, 6)
            def _(f, i=i, ref=ref, target=target, at=at):
                target[i, f] = pack(lambda j: ref[at + i, f, pl.ds(j * 8, 8), :], tiles, lane)

    def px_at(r, f):
        if r < HALO:
            return px_l[r - 2, f]
        if r >= lon + HALO:
            return px_r[r - lon - HALO, f]
        return px[r - HALO, f, 0]

    keep = inside[...]
    for r in range(2, ext - 2):
        u = scale * halo[r, 4, 0]
        v = scale * halo[r, 5, 0]

        @pl.loop(0, 6)
        def _(f, r=r, u=u, v=v):
            c = halo[r, f, 0]
            xs = [halo[r + d, f, 0] for d in (-2, -1, 1, 2)]
            ys = y_shifts(c, px_at(r, f), slot_masks)
            s1_halo[r - 2, f] = keep * stencil(c, xs, ys, u, v)

    @pl.loop(0, tiles)
    def _(t):
        rows = pl.ds(pl.multiple_of(t * 8, 8), 8)
        turn = LANES - (8 * t + 4)

        def at(r, f):
            ref, i = place(r)
            return ref[i, f, rows, :]

        for r in range(2, ext - 2):
            u = scale * at(r, 4)
            v = scale * at(r, 5)
            for f in range(6):
                c = at(r, f)
                xs = [at(r + d, f) for d in (-2, -1, 1, 2)]
                ys = y_shifts(c, pltpu.roll(halo[r, f, 0], turn, 1), masks)
                s1[r - 2, f] = stencil(c, xs, ys, u, v)
        for r in range(2, ext - 6):
            u = scale * s1[r, 4]
            v = scale * s1[r, 5]
            for f in range(6):
                c = s1[r, f]
                xs = [s1[r + d, f] for d in (-2, -1, 1, 2)]
                ys = y_shifts(c, pltpu.roll(s1_halo[r, f], turn, 1), masks)
                adv[f, pl.ds(t * (8 * lon) + (r - 2), 8, stride=lon), :] = stencil(c, xs, ys, u, v)


def local(state, conv_mask, micro_mask, w_in, w_hidden, w_out):
    fields, levels, lon, lat = state.shape
    hid = w_in.shape[0]
    groups = 2
    tiles = -(-levels // (8 * groups))
    pad = groups * tiles * 8
    flat = fields * levels * lon
    cells = state.reshape(flat, lat)
    f32 = jnp.float32
    full = pl.BlockSpec(memory_space=pltpu.VMEM)
    params = pltpu.CompilerParams(vmem_limit_bytes=VMEM_LIMIT)
    scratch = [
        pltpu.VMEM((hid, 4 * lat), jnp.bfloat16),
        pltpu.VMEM((hid, 4 * lat), jnp.bfloat16),
        pltpu.VMEM((-(-w_out.shape[0] // 8) * 8, 4 * lat), f32),
    ]

    def cost(rows):
        return pl.CostEstimate(
            flops=2 * rows * lat * (w_in.size + w_hidden.size + w_out.size),
            bytes_accessed=4 * flat * lat * 2 + 2 * (w_in.size + w_hidden.size + w_out.size),
            transcendentals=3 * rows * lat * (hid + levels),
        )

    edge = jax.ShapeDtypeStruct((HALO, fields, pad, lat), f32)
    lo, hi, tlo, thi = pl.pallas_call(
        functools.partial(edge_kernel, levels, lon),
        out_shape=[edge] * 4,
        in_specs=[full] * 6,
        out_specs=[full] * 4,
        scratch_shapes=scratch,
        compiler_params=params,
        cost_estimate=cost(2 * HALO),
        name="physics_edge",
    )(cells, conv_mask, micro_mask, w_in, w_hidden, w_out)

    def both(axis, up, down, closed):
        n = lax.axis_size(axis)
        ends = n if closed else n - 1
        return (
            lax.ppermute(up, axis, [(i, (i + 1) % n) for i in range(ends)]),
            lax.ppermute(down, axis, [((i + 1) % n, i) for i in range(ends)]),
        )

    left, right = both("col", hi, lo, True)
    mid, tend, px = pl.pallas_call(
        functools.partial(inner_kernel, levels, lon, groups, tiles),
        out_shape=[
            jax.ShapeDtypeStruct((lon - 2 * HALO, fields, pad, lat), f32),
            jax.ShapeDtypeStruct((flat, lat), f32),
            jax.ShapeDtypeStruct((lon, fields, groups, 8, lat), f32),
        ],
        in_specs=[full] * 10,
        out_specs=[full] * 3,
        scratch_shapes=scratch,
        compiler_params=params,
        cost_estimate=cost(lon - 2 * HALO),
        name="physics_inner",
    )(cells, conv_mask, micro_mask, w_in, w_hidden, w_out, lo, hi, tlo, thi)

    before, after = both("row", px, px, False)
    slot = lax.broadcasted_iota(jnp.int32, (8, lat), 1) % 8
    own = jnp.where(slot < 4, before, after)
    corner_l, corner_r = both("col", own[lon - HALO :], own[:HALO], True)
    halo = jnp.concatenate([corner_l, own, corner_r], axis=0)
    row = lax.axis_index("row")
    first, last = row == 0, row == lax.axis_size("row") - 1
    inside = jnp.where(jnp.where(slot < 4, first, last), 0.0, 1.0).astype(f32)

    ext = lon + 2 * HALO

    def rows_spec(n):
        return pl.BlockSpec((n, fields, 8 * tiles, lat), lambda g: (0, 0, g, 0))

    def packed_spec(n):
        return pl.BlockSpec((n, fields, 1, 8, lat), lambda g: (0, 0, g, 0, 0))

    adv = pl.pallas_call(
        functools.partial(advect_kernel, lon, tiles),
        grid=(groups,),
        out_shape=jax.ShapeDtypeStruct((fields, levels * lon, lat), f32),
        in_specs=[
            rows_spec(HALO),
            rows_spec(HALO),
            rows_spec(lon - 2 * HALO),
            rows_spec(HALO),
            rows_spec(HALO),
            packed_spec(lon),
            packed_spec(ext),
            pl.BlockSpec((8, lat), lambda g: (0, 0)),
        ],
        out_specs=pl.BlockSpec((fields, 8 * tiles * lon, lat), lambda g: (0, g, 0)),
        scratch_shapes=[
            pltpu.VMEM((2, fields, 8, lat), f32),
            pltpu.VMEM((2, fields, 8, lat), f32),
            pltpu.VMEM((ext - 4, fields, 8, lat), f32),
            pltpu.VMEM((ext - 4, fields, 8, lat), f32),
        ],
        compiler_params=params,
        cost_estimate=pl.CostEstimate(
            flops=60 * flat * lat, bytes_accessed=12 * flat * lat, transcendentals=0
        ),
        name="advect",
    )(left, lo, mid, hi, right, px, halo, inside)
    return adv.reshape(state.shape), tend.reshape(state.shape)


def solution(mesh):
    in_specs = (P(None, None, "col", "row"), P("col", "row"), P("col", "row"), P(), P(), P())
    out_specs = (P(None, None, "col", "row"), P(None, None, "col", "row"))
    return jax.shard_map(local, mesh=mesh, in_specs=in_specs, out_specs=out_specs, check_vma=False)
```

```python
import functools

import jax
import jax.numpy as jnp
import numpy as np
from jax import lax
from jax.experimental import pallas as pl
from jax.experimental.pallas import tpu as pltpu
from jax.sharding import PartitionSpec as P

ITERS = 3
LANES = 128
HALO = 4
VMEM_LIMIT = 56 * 1024 * 1024


def silu(v):
    half = 0.5 * v
    return half + half * jnp.tanh(half)


def network(z, w_in, w_hidden, w_out, h_a, h_b, out):
    hid = w_in.shape[0]
    part = 256

    def layer(weight, source, target):
        ready = None
        for m in range(0, hid + part, part):
            acc = None
            if m < hid:
                acc = jnp.dot(weight(m), source, preferred_element_type=jnp.float32)
            if ready is not None:
                target[m - part : m, :] = silu(ready).astype(jnp.bfloat16)
            ready = acc

    layer(lambda m: w_in[m : m + part, :], z, h_a)
    layer(lambda m: w_hidden[0, m : m + part, :], h_a[...], h_b)
    layer(lambda m: w_hidden[1, m : m + part, :], h_b[...], h_a)
    out[: w_out.shape[0], :] = jnp.dot(w_out[...], h_a[...], preferred_element_type=jnp.float32)


def saturate(temp, vapour, water):
    temp0, vapour0, water0 = temp, vapour, water
    for _ in range(ITERS):
        satur = 0.5 * jnp.exp(0.5 * temp)
        delta = jnp.maximum(0.5 * (vapour - satur), -water)
        temp = temp + 0.5 * delta
        vapour = vapour - delta
        water = water + delta
    autoconv = 0.6 * jnp.maximum(water - 0.8, 0.0)
    water = water - autoconv
    return temp - temp0, vapour - vapour0, water - water0, autoconv


def physics_rows(rows, levels, lon, state, conv, micro, weights, scr, put):
    w_in, w_hidden, w_out = weights
    h_a, h_b, out = scr

    def field(f, l):
        return state[pl.ds(f * levels * lon + l, levels, stride=lon), :]

    z = jnp.concatenate(
        [state[pl.ds(l, 6 * levels, stride=lon), :].astype(jnp.bfloat16) for l in rows], axis=1
    )
    network(z, w_in, w_hidden, w_out, h_a, h_b, out)
    for k, l in enumerate(rows):
        c = conv[pl.ds(l, 1), :].astype(jnp.float32)
        m = micro[pl.ds(l, 1), :].astype(jnp.float32)
        cols = slice(k * LANES, (k + 1) * LANES)

        def net(f):
            return c * out[f * levels : (f + 1) * levels, cols]

        temp, vapour, water = field(0, l), field(1, l), field(2, l)
        d_t, d_q, d_w, auto = saturate(temp, vapour, water)
        t0 = net(0) + m * d_t
        put(k, 0, temp + t0, t0)
        t1 = net(1) + m * d_q
        put(k, 1, vapour + t1, t1)
        t2 = m * d_w
        put(k, 2, water + t2, t2)
        t3 = m * auto
        put(k, 3, field(3, l) + t3, t3)
        t4 = net(2)
        put(k, 4, field(4, l) + t4, t4)
        t5 = net(3)
        put(k, 5, field(5, l) + t5, t5)


def edge_kernel(levels, lon, state, conv, micro, w_in, w_hidden, w_out, lo, hi, tlo, thi, h_a, h_b, out):
    @pl.loop(0, HALO // 2)
    def _(i):
        blank = jnp.zeros((lo.shape[2] - levels, LANES), jnp.float32)
        rows = [2 * i, 2 * i + 1, lon - HALO + 2 * i, lon - HALO + 2 * i + 1]

        def put(k, f, upd, tend):
            u_ref, t_ref = (lo, tlo) if k < 2 else (hi, thi)
            u_ref[2 * i + k % 2, f, :levels, :] = upd
            u_ref[2 * i + k % 2, f, levels:, :] = blank
            t_ref[2 * i + k % 2, f, :levels, :] = tend

        physics_rows(rows, levels, lon, state, conv, micro, (w_in, w_hidden, w_out), (h_a, h_b, out), put)


def pack(tile, tiles, lane):
    acc = None
    for j in range(tiles):
        turned = pltpu.roll(tile(j), (8 * j + 4) % LANES, 1)
        acc = turned if acc is None else jnp.where(lane // 8 == j, turned, acc)
    return acc


def inner_kernel(
    levels, lon, groups, tiles, state, conv, micro, w_in, w_hidden, w_out, lo, hi, tlo, thi,
    mid, tend, packed, h_a, h_b, out,
):
    @pl.loop(0, (lon - 2 * HALO) // 4)
    def _(i):
        rows = [HALO + 4 * i + k for k in range(4)]
        blank = jnp.zeros((mid.shape[2] - levels, LANES), jnp.float32)

        def put(k, f, upd, tnd):
            mid[4 * i + k, f, :levels, :] = upd
            mid[4 * i + k, f, levels:, :] = blank
            tend[pl.ds(f * levels * lon + rows[k], levels, stride=lon), :] = tnd

        physics_rows(rows, levels, lon, state, conv, micro, (w_in, w_hidden, w_out), (h_a, h_b, out), put)

    @pl.loop(0, HALO)
    def _(i):
        for f in range(6):
            tend[pl.ds(f * levels * lon + i, levels, stride=lon), :] = tlo[i, f, :levels, :]
            tend[pl.ds(f * levels * lon + lon - HALO + i, levels, stride=lon), :] = thi[i, f, :levels, :]

    lane = lax.broadcasted_iota(jnp.int32, (8, LANES), 1)
    for source, first, count in ((lo, 0, HALO), (mid, HALO, lon - 2 * HALO), (hi, lon - HALO, HALO)):

        @pl.loop(0, count)
        def _(i, source=source, first=first):
            for f in range(6):
                for g in range(groups):
                    packed[first + i, f, g] = pack(
                        lambda j: source[i, f, pl.ds((g * tiles + j) * 8, 8), :], tiles, lane
                    )


def split(x):
    high = x.astype(jnp.bfloat16)
    low = (x - high.astype(jnp.float32)).astype(jnp.bfloat16)
    return jnp.concatenate([high, low], axis=-1)


def banded(source, target):
    dist = source[:, None] - target[None, :]
    slope = 8.0 * (dist == 1) - 8.0 * (dist == -1) - 1.0 * (dist == 2) + 1.0 * (dist == -2)
    hyper = 4.0 * (abs(dist) == 1) - 1.0 * (abs(dist) == 2) - 12.0 * (dist == 0)
    half = np.concatenate([slope, hyper], axis=1)
    return half


def twice(half):
    return np.concatenate([half, half], axis=0).astype(jnp.bfloat16)


def matrices(lat, tiles):
    lanes = np.arange(lat)
    slot, group = lanes % 8, lanes // 8
    beyond = np.where(slot < 4, slot - 4, lat + slot - 4)
    own = np.where(slot < 4, lat + slot - 4, slot - 4)
    center = twice(banded(lanes, lanes))
    edges = np.stack([twice(banded(beyond, lanes) * (group == j)[:, None]) for j in range(tiles)])
    same = np.concatenate([group[:, None] == group[None, :]] * 2, axis=1)
    return center, edges, twice(banded(beyond, beyond) * same), twice(banded(own, beyond) * same)


def stencil(center, xs, y, wind_u, wind_v):
    xm2, xm1, xp1, xp2 = xs
    along_x = 8.0 * (xp1 - xm1) - (xp2 - xm2)
    hyper = 4.0 * (xp1 + xm1) - (xp2 + xm2) + y[:, LANES:]
    return center + (wind_u * along_x + wind_v * y[:, :LANES]) + 0.06 * hyper


def winds(center):
    scale = -0.15 / 12.0
    u, v = scale * center[32:40], scale * center[40:48]
    return jnp.concatenate([u] * 6, axis=0), jnp.concatenate([v] * 6, axis=0)


def dot(a, b):
    return jnp.dot(a, b, preferred_element_type=jnp.float32)


def advect_kernel(
    lon, tiles, left, lo, mid, hi, right, px, halo, inside, m_center, m_edges, m_packed, m_own, adv,
    px_side, halo_parts, s1_parts, y, s1,
):
    lane = lax.broadcasted_iota(jnp.int32, (8, LANES), 1)
    ext = lon + 2 * HALO
    n = 48

    def place(r):
        for ref, first, count in (
            (left, 0, HALO),
            (lo, HALO, HALO),
            (mid, 2 * HALO, lon - 2 * HALO),
            (hi, lon, HALO),
            (right, lon + HALO, HALO),
        ):
            if r < first + count:
                return ref, r - first

    for k, (ref, i) in enumerate(((left, 2), (left, 3), (right, 0), (right, 1))):

        @pl.loop(0, 6)
        def _(f, i=i, k=k, ref=ref):
            px_side[k, f] = pack(lambda j: ref[i, f, pl.ds(j * 8, 8), :], tiles, lane)

    def rows_of(a):
        return a.reshape(-1, LANES)

    beyond = rows_of(halo[...])
    halo_parts[...] = split(beyond)
    own = jnp.concatenate([rows_of(px_side[:2]), rows_of(px[...]), rows_of(px_side[2:])], axis=0)
    y[...] = dot(halo_parts[2 * n : (ext - 2) * n, :], m_packed[...]) + dot(split(own), m_own[...])
    keep = jnp.concatenate([inside[...]] * 6, axis=0)
    for r in range(2, ext - 2):
        c = rows_of(halo[r])
        xs = [rows_of(halo[r + d]) for d in (-2, -1, 1, 2)]
        new = keep * stencil(c, xs, y[(r - 2) * n : (r - 1) * n, :], *winds(c))
        s1_parts[(r - 2) * n : (r - 1) * n, :] = split(new)

    @pl.loop(0, tiles)
    def _(t):
        rows = pl.ds(pl.multiple_of(t * 8, 8), 8)

        def at(r):
            ref, i = place(r)
            return rows_of(ref[i, :, rows, :])

        cells = jnp.concatenate([at(r) for r in range(2, ext - 2)], axis=0)
        y[...] = dot(split(cells), m_center[...]) + dot(halo_parts[2 * n : (ext - 2) * n, :], m_edges[t])
        for r in range(2, ext - 2):
            c = at(r)
            xs = [at(r + d) for d in (-2, -1, 1, 2)]
            k = r - 2
            s1[k * n : (k + 1) * n, :] = stencil(c, xs, y[k * n : (k + 1) * n, :], *winds(c))
        last = lon * n
        y[:last, :] = dot(split(s1[2 * n : 2 * n + last, :]), m_center[...]) + dot(
            s1_parts[2 * n : 2 * n + last, :], m_edges[t]
        )
        for r in range(lon):
            c = s1[(r + 2) * n : (r + 3) * n, :]
            xs = [s1[(r + 2 + d) * n : (r + 3 + d) * n, :] for d in (-2, -1, 1, 2)]
            new = stencil(c, xs, y[r * n : (r + 1) * n, :], *winds(c))
            for f in range(6):
                adv[f, pl.ds(t * (8 * lon) + r, 8, stride=lon), :] = new[8 * f : 8 * f + 8]


def local(state, conv_mask, micro_mask, w_in, w_hidden, w_out):
    fields, levels, lon, lat = state.shape
    hid = w_in.shape[0]
    groups = 2
    tiles = -(-levels // (8 * groups))
    pad = groups * tiles * 8
    flat = fields * levels * lon
    cells = state.reshape(flat, lat)
    f32 = jnp.float32
    full = pl.BlockSpec(memory_space=pltpu.VMEM)
    params = pltpu.CompilerParams(vmem_limit_bytes=VMEM_LIMIT)
    scratch = [
        pltpu.VMEM((hid, 4 * lat), jnp.bfloat16),
        pltpu.VMEM((hid, 4 * lat), jnp.bfloat16),
        pltpu.VMEM((-(-w_out.shape[0] // 8) * 8, 4 * lat), f32),
    ]

    def cost(rows):
        return pl.CostEstimate(
            flops=2 * rows * lat * (w_in.size + w_hidden.size + w_out.size),
            bytes_accessed=4 * flat * lat * 2 + 2 * (w_in.size + w_hidden.size + w_out.size),
            transcendentals=3 * rows * lat * (hid + levels),
        )

    edge = jax.ShapeDtypeStruct((HALO, fields, pad, lat), f32)
    lo, hi, tlo, thi = pl.pallas_call(
        functools.partial(edge_kernel, levels, lon),
        out_shape=[edge] * 4,
        in_specs=[full] * 6,
        out_specs=[full] * 4,
        scratch_shapes=scratch,
        compiler_params=params,
        cost_estimate=cost(2 * HALO),
        name="physics_edge",
    )(cells, conv_mask, micro_mask, w_in, w_hidden, w_out)

    def both(axis, up, down, closed):
        n = lax.axis_size(axis)
        ends = n if closed else n - 1
        return (
            lax.ppermute(up, axis, [(i, (i + 1) % n) for i in range(ends)]),
            lax.ppermute(down, axis, [((i + 1) % n, i) for i in range(ends)]),
        )

    left, right = both("col", hi, lo, True)
    mid, tend, px = pl.pallas_call(
        functools.partial(inner_kernel, levels, lon, groups, tiles),
        out_shape=[
            jax.ShapeDtypeStruct((lon - 2 * HALO, fields, pad, lat), f32),
            jax.ShapeDtypeStruct((flat, lat), f32),
            jax.ShapeDtypeStruct((lon, fields, groups, 8, lat), f32),
        ],
        in_specs=[full] * 10,
        out_specs=[full] * 3,
        scratch_shapes=scratch,
        compiler_params=params,
        cost_estimate=cost(lon - 2 * HALO),
        name="physics_inner",
    )(cells, conv_mask, micro_mask, w_in, w_hidden, w_out, lo, hi, tlo, thi)

    before, after = both("row", px, px, False)
    slot = lax.broadcasted_iota(jnp.int32, (8, lat), 1) % 8
    own = jnp.where(slot < 4, before, after)
    corner_l, corner_r = both("col", own[lon - HALO :], own[:HALO], True)
    halo = jnp.concatenate([corner_l, own, corner_r], axis=0)
    row = lax.axis_index("row")
    first, last = row == 0, row == lax.axis_size("row") - 1
    inside = jnp.where(jnp.where(slot < 4, first, last), 0.0, 1.0).astype(f32)

    ext = lon + 2 * HALO
    center, edges, packed, own_edges = (jnp.asarray(m) for m in matrices(lat, tiles))

    def rows_spec(n):
        return pl.BlockSpec((n, fields, 8 * tiles, lat), lambda g: (0, 0, g, 0))

    def packed_spec(n):
        return pl.BlockSpec((n, fields, 1, 8, lat), lambda g: (0, 0, g, 0, 0))

    adv = pl.pallas_call(
        functools.partial(advect_kernel, lon, tiles),
        grid=(groups,),
        out_shape=jax.ShapeDtypeStruct((fields, levels * lon, lat), f32),
        in_specs=[
            rows_spec(HALO),
            rows_spec(HALO),
            rows_spec(lon - 2 * HALO),
            rows_spec(HALO),
            rows_spec(HALO),
            packed_spec(lon),
            packed_spec(ext),
            pl.BlockSpec((8, lat), lambda g: (0, 0)),
            pl.BlockSpec(center.shape, lambda g: (0, 0)),
            pl.BlockSpec(edges.shape, lambda g: (0, 0, 0)),
            pl.BlockSpec(packed.shape, lambda g: (0, 0)),
            pl.BlockSpec(own_edges.shape, lambda g: (0, 0)),
        ],
        out_specs=pl.BlockSpec((fields, 8 * tiles * lon, lat), lambda g: (0, g, 0)),
        scratch_shapes=[
            pltpu.VMEM((4, fields, 8, lat), f32),
            pltpu.VMEM((ext * 48, 2 * lat), jnp.bfloat16),
            pltpu.VMEM(((ext - 4) * 48, 2 * lat), jnp.bfloat16),
            pltpu.VMEM(((ext - 4) * 48, 2 * lat), f32),
            pltpu.VMEM(((ext - 4) * 48, lat), f32),
        ],
        compiler_params=params,
        cost_estimate=pl.CostEstimate(
            flops=60 * flat * lat, bytes_accessed=12 * flat * lat, transcendentals=0
        ),
        name="advect",
    )(left, lo, mid, hi, right, px, halo, inside, center, edges, packed, own_edges)
    return adv.reshape(state.shape), tend.reshape(state.shape)


def solution(mesh):
    in_specs = (P(None, None, "col", "row"), P("col", "row"), P("col", "row"), P(), P(), P())
    out_specs = (P(None, None, "col", "row"), P(None, None, "col", "row"))
    return jax.shard_map(local, mesh=mesh, in_specs=in_specs, out_specs=out_specs, check_vma=False)
```

```python
import functools

import jax
import jax.numpy as jnp
import numpy as np
from jax import lax
from jax.experimental import pallas as pl
from jax.experimental.pallas import tpu as pltpu
from jax.sharding import PartitionSpec as P

ITERS = 3
LANES = 128
HALO = 4


def silu(v):
    half = 0.5 * v
    return half + half * jnp.tanh(half)


def network(z, w_in, w_hidden, w_out, h_a, h_b, out):
    hid = w_in.shape[1]
    part = 256

    def layer(weight, source, target):
        ready = None
        for m in range(0, hid + part, part):
            acc = None
            if m < hid:
                acc = jnp.dot(weight(m), source, preferred_element_type=jnp.float32)
            if ready is not None:
                target[m - part : m, :] = silu(ready).astype(jnp.bfloat16)
            ready = acc

    layer(lambda m: w_in[:, m : m + part].T, z, h_a)
    layer(lambda m: w_hidden[0, m : m + part, :], h_a[...], h_b)
    layer(lambda m: w_hidden[1, m : m + part, :], h_b[...], h_a)
    out[: w_out.shape[0], :] = jnp.dot(w_out[...], h_a[...], preferred_element_type=jnp.float32)


def saturate(temp, vapour, water):
    temp0, vapour0, water0 = temp, vapour, water
    for _ in range(ITERS):
        satur = 0.5 * jnp.exp(0.5 * temp)
        delta = jnp.maximum(0.5 * (vapour - satur), -water)
        temp = temp + 0.5 * delta
        vapour = vapour - delta
        water = water + delta
    autoconv = 0.6 * jnp.maximum(water - 0.8, 0.0)
    water = water - autoconv
    return temp - temp0, vapour - vapour0, water - water0, autoconv


def physics_rows(rows, levels, lon, state, conv, micro, weights, scr, put):
    w_in, w_hidden, w_out = weights
    h_a, h_b, out = scr

    def field(f, l):
        return state[pl.ds(f * levels * lon + l, levels, stride=lon), :]

    z = jnp.concatenate(
        [state[pl.ds(l, 6 * levels, stride=lon), :].astype(jnp.bfloat16) for l in rows], axis=1
    )
    network(z, w_in, w_hidden, w_out, h_a, h_b, out)
    for k, l in enumerate(rows):
        c = conv[pl.ds(l, 1), :].astype(jnp.float32)
        m = micro[pl.ds(l, 1), :].astype(jnp.float32)
        cols = slice(k * LANES, (k + 1) * LANES)

        def net(f):
            return c * out[f * levels : (f + 1) * levels, cols]

        temp, vapour, water = field(0, l), field(1, l), field(2, l)
        d_t, d_q, d_w, auto = saturate(temp, vapour, water)
        t0 = net(0) + m * d_t
        put(k, 0, temp + t0, t0)
        t1 = net(1) + m * d_q
        put(k, 1, vapour + t1, t1)
        t2 = m * d_w
        put(k, 2, water + t2, t2)
        t3 = m * auto
        put(k, 3, field(3, l) + t3, t3)
        t4 = net(2)
        put(k, 4, field(4, l) + t4, t4)
        t5 = net(3)
        put(k, 5, field(5, l) + t5, t5)


def edge_kernel(levels, lon, state, conv, micro, w_in, w_hidden, w_out, lo, hi, tlo, thi, h_a, h_b, out):
    @pl.loop(0, HALO // 2)
    def _(i):
        blank = jnp.zeros((lo.shape[2] - levels, LANES), jnp.float32)
        rows = [2 * i, 2 * i + 1, lon - HALO + 2 * i, lon - HALO + 2 * i + 1]

        def put(k, f, upd, tend):
            u_ref, t_ref = (lo, tlo) if k < 2 else (hi, thi)
            u_ref[2 * i + k % 2, f, :levels, :] = upd
            u_ref[2 * i + k % 2, f, levels:, :] = blank
            t_ref[2 * i + k % 2, f, :levels, :] = tend

        physics_rows(rows, levels, lon, state, conv, micro, (w_in, w_hidden, w_out), (h_a, h_b, out), put)


def pack(tile, tiles, lane):
    acc = None
    for j in range(tiles):
        turned = pltpu.roll(tile(j), (8 * j + 4) % LANES, 1)
        acc = turned if acc is None else jnp.where(lane // 8 == j, turned, acc)
    return acc


def inner_kernel(
    levels, lon, tiles, state, conv, micro, w_in, w_hidden, w_out, lo, hi,
    mid, tmid, packed, q_up, q_down, h_a, h_b, out,
):
    blank = jnp.zeros((mid.shape[2] - levels, LANES), jnp.float32)

    @pl.loop(0, (lon - 2 * HALO) // 4)
    def _(i):
        rows = [HALO + 4 * i + k for k in range(4)]

        def put(k, f, upd, tnd):
            mid[4 * i + k, f, :levels, :] = upd
            mid[4 * i + k, f, levels:, :] = blank
            tmid[4 * i + k, f, :levels, :] = tnd

        physics_rows(rows, levels, lon, state, conv, micro, (w_in, w_hidden, w_out), (h_a, h_b, out), put)

    lane = lax.broadcasted_iota(jnp.int32, (8, LANES), 1)
    lower = lane % 8 < 4
    for source, first, count in ((lo, 0, HALO), (mid, HALO, lon - 2 * HALO), (hi, lon - HALO, HALO)):

        @pl.loop(0, count)
        def _(i, source=source, first=first):
            done = []
            for f in range(6):
                a, b = (
                    pack(lambda j: source[i, f, pl.ds((g * tiles + j) * 8, 8), :], tiles, lane)
                    for g in range(2)
                )
                up = jnp.where(lower, a, pltpu.roll(b, 4, 1))
                down = jnp.where(lower, pltpu.roll(b, LANES - 4, 1), a)
                done.append((a, b, up, down))
            for f, (a, b, up, down) in enumerate(done):
                packed[first + i, f, 0] = a
                packed[first + i, f, 1] = b
                q_up[first + i, f] = up
                q_down[first + i, f] = down


def gather_kernel(levels, lon, tlo, tmid, thi, tend):
    for source, first, count in ((tlo, 0, HALO), (tmid, HALO, lon - 2 * HALO), (thi, lon - HALO, HALO)):

        @pl.loop(0, count)
        def _(i, source=source, first=first):
            got = [source[i, f, :levels, :] for f in range(6)]
            for f in range(6):
                tend[pl.ds(f * levels * lon + first + i, levels, stride=lon), :] = got[f]


def split(x):
    high = x.astype(jnp.bfloat16)
    low = (x - high.astype(jnp.float32)).astype(jnp.bfloat16)
    return jnp.concatenate([high, low], axis=-1)


def banded(source, target):
    dist = source[:, None] - target[None, :]
    slope = 8.0 * (dist == 1) - 8.0 * (dist == -1) - 1.0 * (dist == 2) + 1.0 * (dist == -2)
    hyper = 4.0 * (abs(dist) == 1) - 1.0 * (abs(dist) == 2) - 12.0 * (dist == 0)
    half = np.concatenate([slope, hyper], axis=1)
    return half


def twice(half):
    return np.concatenate([half, half], axis=0).astype(jnp.bfloat16)


def matrices(lat, tiles):
    lanes = np.arange(lat)
    slot, group = lanes % 8, lanes // 8
    own = np.where(slot < 4, lat + slot - 4, slot - 4)
    same = np.concatenate([group[:, None] == group[None, :]] * 2, axis=1)
    edges, packed, owned = [], [], []
    for beyond in (np.where(slot < 4, slot - 4, lat + slot - 4), np.where(slot < 4, lat + slot, slot - 8)):
        edges.append([twice(banded(beyond, lanes) * (group == j)[:, None]) for j in range(tiles)])
        packed.append(twice(banded(beyond, beyond) * same))
        owned.append(twice(banded(own, beyond) * same))
    return twice(banded(lanes, lanes)), np.array(edges), np.array(packed), np.array(owned)


def stencil(center, xs, y, wind_u, wind_v):
    xm2, xm1, xp1, xp2 = xs
    along_x = 8.0 * (xp1 - xm1) - (xp2 - xm2)
    hyper = 4.0 * (xp1 + xm1) - (xp2 + xm2) + y[:, LANES:]
    return center + (wind_u * along_x + wind_v * y[:, :LANES]) + 0.06 * hyper


def winds(center):
    scale = -0.15 / 12.0
    u, v = scale * center[32:40], scale * center[40:48]
    return jnp.concatenate([u] * 6, axis=0), jnp.concatenate([v] * 6, axis=0)


def dot(a, b):
    return jnp.dot(a, b, preferred_element_type=jnp.float32)


def advect_kernel(
    lon, tiles, left, lo, mid, hi, right, px, halo, inside, m_center, m_edges, m_packed, m_own, adv,
    px_side, halo_parts, s1_parts, y, s1,
):
    lane = lax.broadcasted_iota(jnp.int32, (8, LANES), 1)
    ext = lon + 2 * HALO
    n = 48

    def place(r):
        for ref, first, count in (
            (left, 0, HALO),
            (lo, HALO, HALO),
            (mid, 2 * HALO, lon - 2 * HALO),
            (hi, lon, HALO),
            (right, lon + HALO, HALO),
        ):
            if r < first + count:
                return ref, r - first

    for k, (ref, i) in enumerate(((left, 2), (left, 3), (right, 0), (right, 1))):

        @pl.loop(0, 6)
        def _(f, i=i, k=k, ref=ref):
            px_side[k, f] = pack(lambda j: ref[i, f, pl.ds(j * 8, 8), :], tiles, lane)

    def rows_of(a):
        return a.reshape(-1, LANES)

    beyond = rows_of(halo[...])
    halo_parts[...] = split(beyond)
    own = jnp.concatenate([rows_of(px_side[:2]), rows_of(px[...]), rows_of(px_side[2:])], axis=0)
    y[...] = dot(halo_parts[2 * n : (ext - 2) * n, :], m_packed[0]) + dot(split(own), m_own[0])
    keep = jnp.concatenate([inside[0]] * 6, axis=0)
    for r in range(2, ext - 2):
        c = rows_of(halo[r])
        xs = [rows_of(halo[r + d]) for d in (-2, -1, 1, 2)]
        new = keep * stencil(c, xs, y[(r - 2) * n : (r - 1) * n, :], *winds(c))
        s1_parts[(r - 2) * n : (r - 1) * n, :] = split(new)

    @pl.loop(0, tiles)
    def _(t):
        rows = pl.ds(pl.multiple_of(t * 8, 8), 8)

        def at(r):
            ref, i = place(r)
            return rows_of(ref[i, :, rows, :])

        cells = jnp.concatenate([at(r) for r in range(2, ext - 2)], axis=0)
        y[...] = dot(split(cells), m_center[...]) + dot(halo_parts[2 * n : (ext - 2) * n, :], m_edges[0, t])
        for r in range(2, ext - 2):
            c = at(r)
            xs = [at(r + d) for d in (-2, -1, 1, 2)]
            k = r - 2
            s1[k * n : (k + 1) * n, :] = stencil(c, xs, y[k * n : (k + 1) * n, :], *winds(c))
        last = lon * n
        y[:last, :] = dot(split(s1[2 * n : 2 * n + last, :]), m_center[...]) + dot(
            s1_parts[2 * n : 2 * n + last, :], m_edges[0, t]
        )
        for r in range(lon):
            c = s1[(r + 2) * n : (r + 3) * n, :]
            xs = [s1[(r + 2 + d) * n : (r + 3 + d) * n, :] for d in (-2, -1, 1, 2)]
            new = stencil(c, xs, y[r * n : (r + 1) * n, :], *winds(c))
            for f in range(6):
                adv[f, pl.ds(t * (8 * lon) + r, 8, stride=lon), :] = new[8 * f : 8 * f + 8]


def local(state, conv_mask, micro_mask, w_in, w_hidden, w_out):
    fields, levels, lon, lat = state.shape
    hid = w_in.shape[0]
    groups = 2
    tiles = -(-levels // (8 * groups))
    pad = groups * tiles * 8
    flat = fields * levels * lon
    cells = state.reshape(flat, lat)
    f32 = jnp.float32
    full = pl.BlockSpec(memory_space=pltpu.VMEM)

    def limit(mib):
        return pltpu.CompilerParams(vmem_limit_bytes=mib * 1024 * 1024)

    scratch = [
        pltpu.VMEM((hid, 4 * lat), jnp.bfloat16),
        pltpu.VMEM((hid, 4 * lat), jnp.bfloat16),
        pltpu.VMEM((-(-w_out.shape[0] // 8) * 8, 4 * lat), f32),
    ]

    def cost(rows):
        return pl.CostEstimate(
            flops=2 * rows * lat * (w_in.size + w_hidden.size + w_out.size),
            bytes_accessed=4 * flat * lat * 2 + 2 * (w_in.size + w_hidden.size + w_out.size),
            transcendentals=3 * rows * lat * (hid + levels),
        )

    edge = jax.ShapeDtypeStruct((HALO, fields, pad, lat), f32)
    lo, hi, tlo, thi = pl.pallas_call(
        functools.partial(edge_kernel, levels, lon),
        out_shape=[edge] * 4,
        in_specs=[full] * 6,
        out_specs=[full] * 4,
        scratch_shapes=scratch,
        compiler_params=limit(32),
        cost_estimate=cost(2 * HALO),
        name="physics_edge",
    )(cells, conv_mask, micro_mask, w_in.T, w_hidden, w_out)

    def both(axis, up, down, closed):
        n = lax.axis_size(axis)
        ends = n if closed else n - 1
        return (
            lax.ppermute(up, axis, [(i, (i + 1) % n) for i in range(ends)]),
            lax.ppermute(down, axis, [((i + 1) % n, i) for i in range(ends)]),
        )

    left, right = both("col", hi, lo, True)
    row_shape = jax.ShapeDtypeStruct((lon - 2 * HALO, fields, pad, lat), f32)
    q_shape = jax.ShapeDtypeStruct((lon, fields, 8, lat), f32)
    mid, tmid, px, q_up, q_down = pl.pallas_call(
        functools.partial(inner_kernel, levels, lon, tiles),
        out_shape=[
            row_shape,
            row_shape,
            jax.ShapeDtypeStruct((lon, fields, groups, 8, lat), f32),
            q_shape,
            q_shape,
        ],
        in_specs=[full] * 8,
        out_specs=[full] * 5,
        scratch_shapes=scratch,
        compiler_params=limit(36),
        cost_estimate=cost(lon - 2 * HALO),
        name="physics_inner",
    )(cells, conv_mask, micro_mask, w_in.T, w_hidden, w_out, lo, hi)

    before, after = both("row", q_up, q_down, False)
    tend = pl.pallas_call(
        functools.partial(gather_kernel, levels, lon),
        out_shape=jax.ShapeDtypeStruct((flat, lat), f32),
        in_specs=[full] * 3,
        out_specs=full,
        compiler_params=limit(20),
        cost_estimate=pl.CostEstimate(flops=flat * lat, bytes_accessed=8 * flat * lat, transcendentals=0),
        name="gather_tendency",
    )(tlo, tmid, thi)
    lower = lax.broadcasted_iota(jnp.int32, (8, lat), 1) % 8 < 4
    own = jnp.stack([jnp.where(lower, before, after), jnp.where(lower, after, before)], axis=2)
    corner_l, corner_r = both("col", own[lon - HALO :], own[:HALO], True)
    halo = jnp.concatenate([corner_l, own, corner_r], axis=0)
    row = lax.axis_index("row")
    first, last = row == 0, row == lax.axis_size("row") - 1
    outside = jnp.stack([jnp.where(lower, first, last), jnp.where(lower, last, first)])
    inside = jnp.where(outside, 0.0, 1.0).astype(f32)

    ext = lon + 2 * HALO
    center, edges, packed, own_edges = (jnp.asarray(m) for m in matrices(lat, tiles))

    def rows_spec(n):
        return pl.BlockSpec((n, fields, 8 * tiles, lat), lambda g: (0, 0, g, 0))

    def packed_spec(n):
        return pl.BlockSpec((n, fields, 1, 8, lat), lambda g: (0, 0, g, 0, 0))

    adv = pl.pallas_call(
        functools.partial(advect_kernel, lon, tiles),
        grid=(groups,),
        out_shape=jax.ShapeDtypeStruct((fields, levels * lon, lat), f32),
        in_specs=[
            rows_spec(HALO),
            rows_spec(HALO),
            rows_spec(lon - 2 * HALO),
            rows_spec(HALO),
            rows_spec(HALO),
            packed_spec(lon),
            packed_spec(ext),
            pl.BlockSpec((1, 8, lat), lambda g: (g, 0, 0)),
            pl.BlockSpec(center.shape, lambda g: (0, 0)),
            pl.BlockSpec((1,) + edges.shape[1:], lambda g: (g, 0, 0, 0)),
            pl.BlockSpec((1,) + packed.shape[1:], lambda g: (g, 0, 0)),
            pl.BlockSpec((1,) + own_edges.shape[1:], lambda g: (g, 0, 0)),
        ],
        out_specs=pl.BlockSpec((fields, 8 * tiles * lon, lat), lambda g: (0, g, 0)),
        scratch_shapes=[
            pltpu.VMEM((4, fields, 8, lat), f32),
            pltpu.VMEM((ext * 48, 2 * lat), jnp.bfloat16),
            pltpu.VMEM(((ext - 4) * 48, 2 * lat), jnp.bfloat16),
            pltpu.VMEM(((ext - 4) * 48, 2 * lat), f32),
            pltpu.VMEM(((ext - 4) * 48, lat), f32),
        ],
        compiler_params=limit(36),
        cost_estimate=pl.CostEstimate(
            flops=60 * flat * lat, bytes_accessed=12 * flat * lat, transcendentals=0
        ),
        name="advect",
    )(left, lo, mid, hi, right, px, halo, inside, center, edges, packed, own_edges)
    return adv.reshape(state.shape), tend.reshape(state.shape)


def solution(mesh):
    in_specs = (P(None, None, "col", "row"), P("col", "row"), P("col", "row"), P(), P(), P())
    out_specs = (P(None, None, "col", "row"), P(None, None, "col", "row"))
    return jax.shard_map(local, mesh=mesh, in_specs=in_specs, out_specs=out_specs, check_vma=False)
```

```python
import functools

import jax
import jax.numpy as jnp
import numpy as np
from jax import lax
from jax.experimental import pallas as pl
from jax.experimental.pallas import tpu as pltpu
from jax.sharding import PartitionSpec as P

ITERS = 3
LANES = 128
HALO = 4


def silu(v):
    half = 0.5 * v
    return half + half * jnp.tanh(half)


def network(z, w_in, w_hidden, w_out, h_a, h_b, out):
    hid = w_in.shape[1]
    part = 256

    def layer(weight, source, target):
        ready = None
        for m in range(0, hid + part, part):
            acc = None
            if m < hid:
                acc = jnp.dot(weight(m), source, preferred_element_type=jnp.float32)
            if ready is not None:
                target[m - part : m, :] = silu(ready).astype(jnp.bfloat16)
            ready = acc

    layer(lambda m: w_in[:, m : m + part].T, z, h_a)
    layer(lambda m: w_hidden[0, m : m + part, :], h_a[...], h_b)
    layer(lambda m: w_hidden[1, m : m + part, :], h_b[...], h_a)
    out[: w_out.shape[0], :] = jnp.dot(w_out[...], h_a[...], preferred_element_type=jnp.float32)


def saturate(temp, vapour, water):
    temp0, vapour0, water0 = temp, vapour, water
    for _ in range(ITERS):
        satur = 0.5 * jnp.exp(0.5 * temp)
        delta = jnp.maximum(0.5 * (vapour - satur), -water)
        temp = temp + 0.5 * delta
        vapour = vapour - delta
        water = water + delta
    autoconv = 0.6 * jnp.maximum(water - 0.8, 0.0)
    water = water - autoconv
    return temp - temp0, vapour - vapour0, water - water0, autoconv


def physics_rows(rows, levels, lon, state, conv, micro, weights, scr, put):
    w_in, w_hidden, w_out = weights
    h_a, h_b, out = scr

    def field(f, l):
        return state[pl.ds(f * levels * lon + l, levels, stride=lon), :]

    z = jnp.concatenate(
        [state[pl.ds(l, 6 * levels, stride=lon), :].astype(jnp.bfloat16) for l in rows], axis=1
    )
    network(z, w_in, w_hidden, w_out, h_a, h_b, out)
    for k, l in enumerate(rows):
        c = conv[pl.ds(l, 1), :].astype(jnp.float32)
        m = micro[pl.ds(l, 1), :].astype(jnp.float32)
        cols = slice(k * LANES, (k + 1) * LANES)

        def net(f):
            return c * out[f * levels : (f + 1) * levels, cols]

        temp, vapour, water = field(0, l), field(1, l), field(2, l)
        d_t, d_q, d_w, auto = saturate(temp, vapour, water)
        t0 = net(0) + m * d_t
        put(k, 0, temp + t0, t0)
        t1 = net(1) + m * d_q
        put(k, 1, vapour + t1, t1)
        t2 = m * d_w
        put(k, 2, water + t2, t2)
        t3 = m * auto
        put(k, 3, field(3, l) + t3, t3)
        t4 = net(2)
        put(k, 4, field(4, l) + t4, t4)
        t5 = net(3)
        put(k, 5, field(5, l) + t5, t5)


def edge_kernel(levels, lon, state, conv, micro, w_in, w_hidden, w_out, lo, hi, tlo, thi, h_a, h_b, out):
    @pl.loop(0, HALO // 2)
    def _(i):
        blank = jnp.zeros((lo.shape[2] - levels, LANES), jnp.float32)
        rows = [2 * i, 2 * i + 1, lon - HALO + 2 * i, lon - HALO + 2 * i + 1]

        def put(k, f, upd, tend):
            u_ref, t_ref = (lo, tlo) if k < 2 else (hi, thi)
            u_ref[2 * i + k % 2, f, :levels, :] = upd
            u_ref[2 * i + k % 2, f, levels:, :] = blank
            t_ref[2 * i + k % 2, f, :levels, :] = tend

        physics_rows(rows, levels, lon, state, conv, micro, (w_in, w_hidden, w_out), (h_a, h_b, out), put)


def pack(tile, tiles, lane):
    acc = None
    for j in range(tiles):
        turned = pltpu.roll(tile(j), (8 * j + 4) % LANES, 1)
        acc = turned if acc is None else jnp.where(lane // 8 == j, turned, acc)
    return acc


def inner_kernel(
    levels, lon, tiles, state, conv, micro, w_in, w_hidden, w_out, _edges,
    mid, tmid, packed, q_up, q_down, h_a, h_b, out,
):
    blank = jnp.zeros((mid.shape[2] - levels, LANES), jnp.float32)

    @pl.loop(0, (lon - 2 * HALO) // 4)
    def _(i):
        rows = [HALO + 4 * i + k for k in range(4)]

        def put(k, f, upd, tnd):
            mid[4 * i + k, f, :levels, :] = upd
            mid[4 * i + k, f, levels:, :] = blank
            tmid[4 * i + k, f, :levels, :] = tnd

        physics_rows(rows, levels, lon, state, conv, micro, (w_in, w_hidden, w_out), (h_a, h_b, out), put)

    pack_rows(mid, 0, lon - 2 * HALO, tiles, packed, q_up, q_down)


def pack_rows(source, first, count, tiles, packed, q_up, q_down):
    lane = lax.broadcasted_iota(jnp.int32, (8, LANES), 1)
    lower = lane % 8 < 4

    @pl.loop(0, count)
    def _(i):
        done = []
        for f in range(6):
            a, b = (
                pack(lambda j: source[i, f, pl.ds((g * tiles + j) * 8, 8), :], tiles, lane)
                for g in range(2)
            )
            up = jnp.where(lower, a, pltpu.roll(b, 4, 1))
            down = jnp.where(lower, pltpu.roll(b, LANES - 4, 1), a)
            done.append((a, b, up, down))
        for f, (a, b, up, down) in enumerate(done):
            packed[first + i, f, 0] = a
            packed[first + i, f, 1] = b
            q_up[first + i, f] = up
            q_down[first + i, f] = down


def pack_kernel(tiles, lo, hi, packed, q_up, q_down):
    pack_rows(lo, 0, HALO, tiles, packed, q_up, q_down)
    pack_rows(hi, HALO, HALO, tiles, packed, q_up, q_down)


def gather_kernel(levels, lon, tlo, tmid, thi, tend):
    for source, first, count in ((tlo, 0, HALO), (tmid, HALO, lon - 2 * HALO), (thi, lon - HALO, HALO)):

        @pl.loop(0, count)
        def _(i, source=source, first=first):
            got = [source[i, f, :levels, :] for f in range(6)]
            for f in range(6):
                tend[pl.ds(f * levels * lon + first + i, levels, stride=lon), :] = got[f]


def split(x):
    high = x.astype(jnp.bfloat16)
    low = (x - high.astype(jnp.float32)).astype(jnp.bfloat16)
    return jnp.concatenate([high, low], axis=-1)


def banded(source, target):
    dist = source[:, None] - target[None, :]
    slope = 8.0 * (dist == 1) - 8.0 * (dist == -1) - 1.0 * (dist == 2) + 1.0 * (dist == -2)
    hyper = 4.0 * (abs(dist) == 1) - 1.0 * (abs(dist) == 2) - 12.0 * (dist == 0)
    half = np.concatenate([slope, hyper], axis=1)
    return half


def twice(half):
    return np.concatenate([half, half], axis=0).astype(jnp.bfloat16)


def matrices(lat, tiles):
    lanes = np.arange(lat)
    slot, group = lanes % 8, lanes // 8
    own = np.where(slot < 4, lat + slot - 4, slot - 4)
    same = np.concatenate([group[:, None] == group[None, :]] * 2, axis=1)
    edges, packed, owned = [], [], []
    for beyond in (np.where(slot < 4, slot - 4, lat + slot - 4), np.where(slot < 4, lat + slot, slot - 8)):
        edges.append([twice(banded(beyond, lanes) * (group == j)[:, None]) for j in range(tiles)])
        packed.append(twice(banded(beyond, beyond) * same))
        owned.append(twice(banded(own, beyond) * same))
    return twice(banded(lanes, lanes)), np.array(edges), np.array(packed), np.array(owned)


def stencil(center, xs, y, wind_u, wind_v):
    xm2, xm1, xp1, xp2 = xs
    along_x = 8.0 * (xp1 - xm1) - (xp2 - xm2)
    hyper = 4.0 * (xp1 + xm1) - (xp2 + xm2) + y[:, LANES:]
    return center + (wind_u * along_x + wind_v * y[:, :LANES]) + 0.06 * hyper


def winds(center):
    scale = -0.15 / 12.0
    u, v = scale * center[32:40], scale * center[40:48]
    return jnp.concatenate([u] * 6, axis=0), jnp.concatenate([v] * 6, axis=0)


def dot(a, b):
    return jnp.dot(a, b, preferred_element_type=jnp.float32)


def advect_kernel(
    lon, tiles, left, lo, mid, hi, right, px_edge, px_mid, halo, inside, m_center, m_edges, m_packed, m_own, adv,
    px_side, halo_parts, s1_parts, y, s1,
):
    lane = lax.broadcasted_iota(jnp.int32, (8, LANES), 1)
    ext = lon + 2 * HALO
    n = 48

    def place(r):
        for ref, first, count in (
            (left, 0, HALO),
            (lo, HALO, HALO),
            (mid, 2 * HALO, lon - 2 * HALO),
            (hi, lon, HALO),
            (right, lon + HALO, HALO),
        ):
            if r < first + count:
                return ref, r - first

    for k, (ref, i) in enumerate(((left, 2), (left, 3), (right, 0), (right, 1))):

        @pl.loop(0, 6)
        def _(f, i=i, k=k, ref=ref):
            px_side[k, f] = pack(lambda j: ref[i, f, pl.ds(j * 8, 8), :], tiles, lane)

    def rows_of(a):
        return a.reshape(-1, LANES)

    beyond = rows_of(halo[...])
    halo_parts[...] = split(beyond)
    own = jnp.concatenate([rows_of(px_side[:2]), rows_of(px_edge[:HALO]), rows_of(px_mid[...]),
         rows_of(px_edge[HALO:]), rows_of(px_side[2:])], axis=0)
    y[...] = dot(halo_parts[2 * n : (ext - 2) * n, :], m_packed[0]) + dot(split(own), m_own[0])
    keep = jnp.concatenate([inside[0]] * 6, axis=0)
    for r in range(2, ext - 2):
        c = rows_of(halo[r])
        xs = [rows_of(halo[r + d]) for d in (-2, -1, 1, 2)]
        new = keep * stencil(c, xs, y[(r - 2) * n : (r - 1) * n, :], *winds(c))
        s1_parts[(r - 2) * n : (r - 1) * n, :] = split(new)

    @pl.loop(0, tiles)
    def _(t):
        rows = pl.ds(pl.multiple_of(t * 8, 8), 8)

        def at(r):
            ref, i = place(r)
            return rows_of(ref[i, :, rows, :])

        cells = jnp.concatenate([at(r) for r in range(2, ext - 2)], axis=0)
        y[...] = dot(split(cells), m_center[...]) + dot(halo_parts[2 * n : (ext - 2) * n, :], m_edges[0, t])
        for r in range(2, ext - 2):
            c = at(r)
            xs = [at(r + d) for d in (-2, -1, 1, 2)]
            k = r - 2
            s1[k * n : (k + 1) * n, :] = stencil(c, xs, y[k * n : (k + 1) * n, :], *winds(c))
        last = lon * n
        y[:last, :] = dot(split(s1[2 * n : 2 * n + last, :]), m_center[...]) + dot(
            s1_parts[2 * n : 2 * n + last, :], m_edges[0, t]
        )
        for r in range(lon):
            c = s1[(r + 2) * n : (r + 3) * n, :]
            xs = [s1[(r + 2 + d) * n : (r + 3 + d) * n, :] for d in (-2, -1, 1, 2)]
            new = stencil(c, xs, y[r * n : (r + 1) * n, :], *winds(c))
            for f in range(6):
                adv[f, pl.ds(t * (8 * lon) + r, 8, stride=lon), :] = new[8 * f : 8 * f + 8]


def local(state, conv_mask, micro_mask, w_in, w_hidden, w_out):
    fields, levels, lon, lat = state.shape
    hid = w_in.shape[0]
    groups = 2
    tiles = -(-levels // (8 * groups))
    pad = groups * tiles * 8
    flat = fields * levels * lon
    cells = state.reshape(flat, lat)
    f32 = jnp.float32
    full = pl.BlockSpec(memory_space=pltpu.VMEM)

    def limit(mib):
        return pltpu.CompilerParams(vmem_limit_bytes=mib * 1024 * 1024)

    scratch = [
        pltpu.VMEM((hid, 4 * lat), jnp.bfloat16),
        pltpu.VMEM((hid, 4 * lat), jnp.bfloat16),
        pltpu.VMEM((-(-w_out.shape[0] // 8) * 8, 4 * lat), f32),
    ]

    def cost(rows):
        return pl.CostEstimate(
            flops=2 * rows * lat * (w_in.size + w_hidden.size + w_out.size),
            bytes_accessed=4 * flat * lat * 2 + 2 * (w_in.size + w_hidden.size + w_out.size),
            transcendentals=3 * rows * lat * (hid + levels),
        )

    edge = jax.ShapeDtypeStruct((HALO, fields, pad, lat), f32)
    lo, hi, tlo, thi = pl.pallas_call(
        functools.partial(edge_kernel, levels, lon),
        out_shape=[edge] * 4,
        in_specs=[full] * 6,
        out_specs=[full] * 4,
        scratch_shapes=scratch,
        compiler_params=limit(56),
        cost_estimate=cost(2 * HALO),
        name="physics_edge",
    )(cells, conv_mask, micro_mask, w_in.T, w_hidden, w_out)

    def both(axis, up, down, closed):
        n = lax.axis_size(axis)
        ends = n if closed else n - 1
        return (
            lax.ppermute(up, axis, [(i, (i + 1) % n) for i in range(ends)]),
            lax.ppermute(down, axis, [((i + 1) % n, i) for i in range(ends)]),
        )

    left, right = both("col", hi, lo, True)
    def packed_shapes(n):
        q = jax.ShapeDtypeStruct((n, fields, 8, lat), f32)
        return [jax.ShapeDtypeStruct((n, fields, groups, 8, lat), f32), q, q]

    px_edge, qe_up, qe_down = pl.pallas_call(
        functools.partial(pack_kernel, tiles),
        out_shape=packed_shapes(2 * HALO),
        in_specs=[full] * 2,
        out_specs=[full] * 3,
        compiler_params=limit(20),
        name="pack_edges",
    )(lo, hi)
    before_e, after_e = both("row", qe_up, qe_down, False)
    row_shape = jax.ShapeDtypeStruct((lon - 2 * HALO, fields, pad, lat), f32)
    mid, tmid, px_mid, q_up, q_down = pl.pallas_call(
        functools.partial(inner_kernel, levels, lon, tiles),
        out_shape=[
            row_shape,
            row_shape,
            *packed_shapes(lon - 2 * HALO),
        ],
        in_specs=[full] * 6 + [pl.BlockSpec(memory_space=pl.ANY)],
        out_specs=[full] * 5,
        scratch_shapes=scratch,
        compiler_params=limit(56),
        cost_estimate=cost(lon - 2 * HALO),
        name="physics_inner",
    )(cells, conv_mask, micro_mask, w_in.T, w_hidden, w_out, px_edge)

    before, after = both("row", q_up, q_down, False)
    tend = pl.pallas_call(
        functools.partial(gather_kernel, levels, lon),
        out_shape=jax.ShapeDtypeStruct((flat, lat), f32),
        in_specs=[full] * 3,
        out_specs=full,
        compiler_params=limit(20),
        cost_estimate=pl.CostEstimate(flops=flat * lat, bytes_accessed=8 * flat * lat, transcendentals=0),
        name="gather_tendency",
    )(tlo, tmid, thi)
    lower = lax.broadcasted_iota(jnp.int32, (8, lat), 1) % 8 < 4

    def joined(before, after):
        return jnp.stack([jnp.where(lower, before, after), jnp.where(lower, after, before)], axis=2)

    own_e = joined(before_e, after_e)
    corner_l, corner_r = both("col", own_e[HALO:], own_e[:HALO], True)
    halo = jnp.concatenate([corner_l, own_e[:HALO], joined(before, after), own_e[HALO:], corner_r], axis=0)
    row = lax.axis_index("row")
    first, last = row == 0, row == lax.axis_size("row") - 1
    outside = jnp.stack([jnp.where(lower, first, last), jnp.where(lower, last, first)])
    inside = jnp.where(outside, 0.0, 1.0).astype(f32)

    ext = lon + 2 * HALO
    center, edges, packed, own_edges = (jnp.asarray(m) for m in matrices(lat, tiles))

    def rows_spec(n):
        return pl.BlockSpec((n, fields, 8 * tiles, lat), lambda g: (0, 0, g, 0))

    def packed_spec(n):
        return pl.BlockSpec((n, fields, 1, 8, lat), lambda g: (0, 0, g, 0, 0))

    adv = pl.pallas_call(
        functools.partial(advect_kernel, lon, tiles),
        grid=(groups,),
        out_shape=jax.ShapeDtypeStruct((fields, levels * lon, lat), f32),
        in_specs=[
            rows_spec(HALO),
            rows_spec(HALO),
            rows_spec(lon - 2 * HALO),
            rows_spec(HALO),
            rows_spec(HALO),
            packed_spec(2 * HALO),
            packed_spec(lon - 2 * HALO),
            packed_spec(ext),
            pl.BlockSpec((1, 8, lat), lambda g: (g, 0, 0)),
            pl.BlockSpec(center.shape, lambda g: (0, 0)),
            pl.BlockSpec((1,) + edges.shape[1:], lambda g: (g, 0, 0, 0)),
            pl.BlockSpec((1,) + packed.shape[1:], lambda g: (g, 0, 0)),
            pl.BlockSpec((1,) + own_edges.shape[1:], lambda g: (g, 0, 0)),
        ],
        out_specs=pl.BlockSpec((fields, 8 * tiles * lon, lat), lambda g: (0, g, 0)),
        scratch_shapes=[
            pltpu.VMEM((4, fields, 8, lat), f32),
            pltpu.VMEM((ext * 48, 2 * lat), jnp.bfloat16),
            pltpu.VMEM(((ext - 4) * 48, 2 * lat), jnp.bfloat16),
            pltpu.VMEM(((ext - 4) * 48, 2 * lat), f32),
            pltpu.VMEM(((ext - 4) * 48, lat), f32),
        ],
        compiler_params=limit(56),
        cost_estimate=pl.CostEstimate(
            flops=60 * flat * lat, bytes_accessed=12 * flat * lat, transcendentals=0
        ),
        name="advect",
    )(left, lo, mid, hi, right, px_edge, px_mid, halo, inside, center, edges, packed, own_edges)
    return adv.reshape(state.shape), tend.reshape(state.shape)


def solution(mesh):
    in_specs = (P(None, None, "col", "row"), P("col", "row"), P("col", "row"), P(), P(), P())
    out_specs = (P(None, None, "col", "row"), P(None, None, "col", "row"))
    return jax.shard_map(local, mesh=mesh, in_specs=in_specs, out_specs=out_specs, check_vma=False)
```

```python
import functools

import jax
import jax.numpy as jnp
import numpy as np
from jax import lax
from jax.experimental import pallas as pl
from jax.experimental.pallas import tpu as pltpu
from jax.sharding import PartitionSpec as P

ITERS = 3
LANES = 128
HALO = 4


def silu(v):
    half = 0.5 * v
    return half + half * jnp.tanh(half)


def network(z, w_in, w_hidden, w_out, h_a, h_b, out):
    hid = w_in.shape[1]
    part = 256

    def layer(weight, source, target):
        ready = None
        for m in range(0, hid + part, part):
            acc = None
            if m < hid:
                acc = jnp.dot(weight(m), source, preferred_element_type=jnp.float32)
            if ready is not None:
                target[m - part : m, :] = silu(ready).astype(jnp.bfloat16)
            ready = acc

    layer(lambda m: w_in[:, m : m + part].T, z, h_a)
    layer(lambda m: w_hidden[0, m : m + part, :], h_a[...], h_b)
    layer(lambda m: w_hidden[1, m : m + part, :], h_b[...], h_a)
    out[: w_out.shape[0], :] = jnp.dot(w_out[...], h_a[...], preferred_element_type=jnp.float32)


def saturate(temp, vapour, water):
    temp0, vapour0, water0 = temp, vapour, water
    for _ in range(ITERS):
        satur = 0.5 * jnp.exp(0.5 * temp)
        delta = jnp.maximum(0.5 * (vapour - satur), -water)
        temp = temp + 0.5 * delta
        vapour = vapour - delta
        water = water + delta
    autoconv = 0.6 * jnp.maximum(water - 0.8, 0.0)
    water = water - autoconv
    return temp - temp0, vapour - vapour0, water - water0, autoconv


def physics_rows(rows, levels, lon, state, conv, micro, weights, scr, put):
    w_in, w_hidden, w_out = weights
    h_a, h_b, out = scr

    def field(f, l):
        return state[pl.ds(f * levels * lon + l, levels, stride=lon), :]

    z = jnp.concatenate(
        [state[pl.ds(l, 6 * levels, stride=lon), :].astype(jnp.bfloat16) for l in rows], axis=1
    )
    network(z, w_in, w_hidden, w_out, h_a, h_b, out)
    for k, l in enumerate(rows):
        c = conv[pl.ds(l, 1), :].astype(jnp.float32)
        m = micro[pl.ds(l, 1), :].astype(jnp.float32)
        cols = slice(k * LANES, (k + 1) * LANES)

        def net(f):
            return c * out[f * levels : (f + 1) * levels, cols]

        temp, vapour, water = field(0, l), field(1, l), field(2, l)
        d_t, d_q, d_w, auto = saturate(temp, vapour, water)
        t0 = net(0) + m * d_t
        put(k, 0, temp + t0, t0)
        t1 = net(1) + m * d_q
        put(k, 1, vapour + t1, t1)
        t2 = m * d_w
        put(k, 2, water + t2, t2)
        t3 = m * auto
        put(k, 3, field(3, l) + t3, t3)
        t4 = net(2)
        put(k, 4, field(4, l) + t4, t4)
        t5 = net(3)
        put(k, 5, field(5, l) + t5, t5)


def edge_kernel(levels, lon, state, conv, micro, w_in, w_hidden, w_out, lo, hi, tlo, thi, h_a, h_b, out):
    @pl.loop(0, HALO // 2)
    def _(i):
        blank = jnp.zeros((lo.shape[2] - levels, LANES), jnp.float32)
        rows = [2 * i, 2 * i + 1, lon - HALO + 2 * i, lon - HALO + 2 * i + 1]

        def put(k, f, upd, tend):
            u_ref, t_ref = (lo, tlo) if k < 2 else (hi, thi)
            u_ref[2 * i + k % 2, f, :levels, :] = upd
            u_ref[2 * i + k % 2, f, levels:, :] = blank
            t_ref[2 * i + k % 2, f, :levels, :] = tend

        physics_rows(rows, levels, lon, state, conv, micro, (w_in, w_hidden, w_out), (h_a, h_b, out), put)


def pack(tile, tiles, lane):
    acc = None
    for j in range(tiles):
        turned = pltpu.roll(tile(j), (8 * j + 4) % LANES, 1)
        acc = turned if acc is None else jnp.where(lane // 8 == j, turned, acc)
    return acc


def inner_kernel(
    levels, lon, tiles, state, conv, micro, w_in, w_hidden, w_out, lo, hi,
    mid, tmid, packed, q_up, q_down, h_a, h_b, out,
):
    blank = jnp.zeros((mid.shape[2] - levels, LANES), jnp.float32)

    @pl.loop(0, (lon - 2 * HALO) // 4)
    def _(i):
        rows = [HALO + 4 * i + k for k in range(4)]

        def put(k, f, upd, tnd):
            mid[4 * i + k, f, :levels, :] = upd
            mid[4 * i + k, f, levels:, :] = blank
            tmid[4 * i + k, f, :levels, :] = tnd

        physics_rows(rows, levels, lon, state, conv, micro, (w_in, w_hidden, w_out), (h_a, h_b, out), put)

    lane = lax.broadcasted_iota(jnp.int32, (8, LANES), 1)
    lower = lane % 8 < 4
    for source, first, count in ((lo, 0, HALO), (mid, HALO, lon - 2 * HALO), (hi, lon - HALO, HALO)):

        @pl.loop(0, count)
        def _(i, source=source, first=first):
            done = []
            for f in range(6):
                a, b = (
                    pack(lambda j: source[i, f, pl.ds((g * tiles + j) * 8, 8), :], tiles, lane)
                    for g in range(2)
                )
                up = jnp.where(lower, a, pltpu.roll(b, 4, 1))
                down = jnp.where(lower, pltpu.roll(b, LANES - 4, 1), a)
                done.append((a, b, up, down))
            for f, (a, b, up, down) in enumerate(done):
                packed[first + i, f, 0] = a
                packed[first + i, f, 1] = b
                q_up[first + i, f] = up
                q_down[first + i, f] = down


def gather_kernel(levels, lon, tlo, tmid, thi, tend):
    for source, first, count in ((tlo, 0, HALO), (tmid, HALO, lon - 2 * HALO), (thi, lon - HALO, HALO)):

        @pl.loop(0, count)
        def _(i, source=source, first=first):
            got = [source[i, f, :levels, :] for f in range(6)]
            for f in range(6):
                tend[pl.ds(f * levels * lon + first + i, levels, stride=lon), :] = got[f]


def split(x):
    high = x.astype(jnp.bfloat16)
    low = (x - high.astype(jnp.float32)).astype(jnp.bfloat16)
    return jnp.concatenate([high, low], axis=-1)


def banded(source, target):
    dist = source[:, None] - target[None, :]
    slope = 8.0 * (dist == 1) - 8.0 * (dist == -1) - 1.0 * (dist == 2) + 1.0 * (dist == -2)
    hyper = 4.0 * (abs(dist) == 1) - 1.0 * (abs(dist) == 2) - 12.0 * (dist == 0)
    half = np.concatenate([slope, hyper], axis=1)
    return half


def twice(half):
    return np.concatenate([half, half], axis=0).astype(jnp.bfloat16)


def matrices(lat, tiles):
    lanes = np.arange(lat)
    slot, group = lanes % 8, lanes // 8
    own = np.where(slot < 4, lat + slot - 4, slot - 4)
    same = np.concatenate([group[:, None] == group[None, :]] * 2, axis=1)
    edges, packed, owned = [], [], []
    for beyond in (np.where(slot < 4, slot - 4, lat + slot - 4), np.where(slot < 4, lat + slot, slot - 8)):
        edges.append([twice(banded(beyond, lanes) * (group == j)[:, None]) for j in range(tiles)])
        packed.append(twice(banded(beyond, beyond) * same))
        owned.append(twice(banded(own, beyond) * same))
    return twice(banded(lanes, lanes)), np.array(edges), np.array(packed), np.array(owned)


def stencil(center, xs, y, wind_u, wind_v):
    xm2, xm1, xp1, xp2 = xs
    along_x = 8.0 * (xp1 - xm1) - (xp2 - xm2)
    hyper = 4.0 * (xp1 + xm1) - (xp2 + xm2) + y[:, LANES:]
    return center + (wind_u * along_x + wind_v * y[:, :LANES]) + 0.06 * hyper


def winds(center):
    scale = -0.15 / 12.0
    u, v = scale * center[32:40], scale * center[40:48]
    return jnp.concatenate([u] * 6, axis=0), jnp.concatenate([v] * 6, axis=0)


def dot(a, b):
    return jnp.dot(a, b, preferred_element_type=jnp.float32)


def advect_kernel(
    lon, tiles, left, lo, mid, hi, right, px, halo, inside, m_center, m_edges, m_packed, m_own, adv,
    px_side, halo_parts, s1_parts, y, s1,
):
    lane = lax.broadcasted_iota(jnp.int32, (8, LANES), 1)
    ext = lon + 2 * HALO
    n = 48

    def place(r):
        for ref, first, count in (
            (left, 0, HALO),
            (lo, HALO, HALO),
            (mid, 2 * HALO, lon - 2 * HALO),
            (hi, lon, HALO),
            (right, lon + HALO, HALO),
        ):
            if r < first + count:
                return ref, r - first

    for k, (ref, i) in enumerate(((left, 2), (left, 3), (right, 0), (right, 1))):

        @pl.loop(0, 6)
        def _(f, i=i, k=k, ref=ref):
            px_side[k, f] = pack(lambda j: ref[i, f, pl.ds(j * 8, 8), :], tiles, lane)

    def rows_of(a):
        return a.reshape(-1, LANES)

    beyond = rows_of(halo[...])
    halo_parts[...] = split(beyond)
    own = jnp.concatenate([rows_of(px_side[:2]), rows_of(px[...]), rows_of(px_side[2:])], axis=0)
    y[...] = dot(halo_parts[2 * n : (ext - 2) * n, :], m_packed[0]) + dot(split(own), m_own[0])
    keep = jnp.concatenate([inside[0]] * 6, axis=0)
    for r in range(2, ext - 2):
        c = rows_of(halo[r])
        xs = [rows_of(halo[r + d]) for d in (-2, -1, 1, 2)]
        new = keep * stencil(c, xs, y[(r - 2) * n : (r - 1) * n, :], *winds(c))
        s1_parts[(r - 2) * n : (r - 1) * n, :] = split(new)

    @pl.loop(0, tiles)
    def _(t):
        rows = pl.ds(pl.multiple_of(t * 8, 8), 8)

        def at(r):
            ref, i = place(r)
            return rows_of(ref[i, :, rows, :])

        cells = jnp.concatenate([at(r) for r in range(2, ext - 2)], axis=0)
        y[...] = dot(split(cells), m_center[...]) + dot(halo_parts[2 * n : (ext - 2) * n, :], m_edges[0, t])
        for r in range(2, ext - 2):
            c = at(r)
            xs = [at(r + d) for d in (-2, -1, 1, 2)]
            k = r - 2
            s1[k * n : (k + 1) * n, :] = stencil(c, xs, y[k * n : (k + 1) * n, :], *winds(c))
        last = lon * n
        y[:last, :] = dot(split(s1[2 * n : 2 * n + last, :]), m_center[...]) + dot(
            s1_parts[2 * n : 2 * n + last, :], m_edges[0, t]
        )
        for r in range(lon):
            c = s1[(r + 2) * n : (r + 3) * n, :]
            xs = [s1[(r + 2 + d) * n : (r + 3 + d) * n, :] for d in (-2, -1, 1, 2)]
            new = stencil(c, xs, y[r * n : (r + 1) * n, :], *winds(c))
            for f in range(6):
                adv[f, pl.ds(t * (8 * lon) + r, 8, stride=lon), :] = new[8 * f : 8 * f + 8]


def local(state, conv_mask, micro_mask, w_in, w_hidden, w_out):
    fields, levels, lon, lat = state.shape
    hid = w_in.shape[0]
    groups = 2
    tiles = -(-levels // (8 * groups))
    pad = groups * tiles * 8
    flat = fields * levels * lon
    cells = state.reshape(flat, lat)
    f32 = jnp.float32
    full = pl.BlockSpec(memory_space=pltpu.VMEM)

    def limit(mib):
        return pltpu.CompilerParams(vmem_limit_bytes=mib * 1024 * 1024)

    scratch = [
        pltpu.VMEM((hid, 4 * lat), jnp.bfloat16),
        pltpu.VMEM((hid, 4 * lat), jnp.bfloat16),
        pltpu.VMEM((-(-w_out.shape[0] // 8) * 8, 4 * lat), f32),
    ]

    def cost(rows):
        return pl.CostEstimate(
            flops=2 * rows * lat * (w_in.size + w_hidden.size + w_out.size),
            bytes_accessed=4 * flat * lat * 2 + 2 * (w_in.size + w_hidden.size + w_out.size),
            transcendentals=3 * rows * lat * (hid + levels),
        )

    edge = jax.ShapeDtypeStruct((HALO, fields, pad, lat), f32)
    lo, hi, tlo, thi = pl.pallas_call(
        functools.partial(edge_kernel, levels, lon),
        out_shape=[edge] * 4,
        in_specs=[full] * 6,
        out_specs=[full] * 4,
        scratch_shapes=scratch,
        compiler_params=limit(56),
        cost_estimate=cost(2 * HALO),
        name="physics_edge",
    )(cells, conv_mask, micro_mask, w_in.T, w_hidden, w_out)

    def both(axis, up, down, closed):
        n = lax.axis_size(axis)
        ends = n if closed else n - 1
        return (
            lax.ppermute(up, axis, [(i, (i + 1) % n) for i in range(ends)]),
            lax.ppermute(down, axis, [((i + 1) % n, i) for i in range(ends)]),
        )

    left, right = both("col", hi, lo, True)
    row_shape = jax.ShapeDtypeStruct((lon - 2 * HALO, fields, pad, lat), f32)
    q_shape = jax.ShapeDtypeStruct((lon, fields, 8, lat), f32)
    mid, tmid, px, q_up, q_down = pl.pallas_call(
        functools.partial(inner_kernel, levels, lon, tiles),
        out_shape=[
            row_shape,
            row_shape,
            jax.ShapeDtypeStruct((lon, fields, groups, 8, lat), f32),
            q_shape,
            q_shape,
        ],
        in_specs=[full] * 8,
        out_specs=[full] * 5,
        scratch_shapes=scratch,
        compiler_params=limit(56),
        cost_estimate=cost(lon - 2 * HALO),
        name="physics_inner",
    )(cells, conv_mask, micro_mask, w_in.T, w_hidden, w_out, lo, hi)

    before, after = both("row", q_up, q_down, False)
    tend = pl.pallas_call(
        functools.partial(gather_kernel, levels, lon),
        out_shape=jax.ShapeDtypeStruct((flat, lat), f32),
        in_specs=[full] * 3,
        out_specs=full,
        compiler_params=limit(20),
        cost_estimate=pl.CostEstimate(flops=flat * lat, bytes_accessed=8 * flat * lat, transcendentals=0),
        name="gather_tendency",
    )(tlo, tmid, thi)
    lower = lax.broadcasted_iota(jnp.int32, (8, lat), 1) % 8 < 4
    own = jnp.stack([jnp.where(lower, before, after), jnp.where(lower, after, before)], axis=2)
    corner_l, corner_r = both("col", own[lon - HALO :], own[:HALO], True)
    halo = jnp.concatenate([corner_l, own, corner_r], axis=0)
    row = lax.axis_index("row")
    first, last = row == 0, row == lax.axis_size("row") - 1
    outside = jnp.stack([jnp.where(lower, first, last), jnp.where(lower, last, first)])
    inside = jnp.where(outside, 0.0, 1.0).astype(f32)

    ext = lon + 2 * HALO
    center, edges, packed, own_edges = (jnp.asarray(m) for m in matrices(lat, tiles))

    def rows_spec(n):
        return pl.BlockSpec((n, fields, 8 * tiles, lat), lambda g: (0, 0, g, 0))

    def packed_spec(n):
        return pl.BlockSpec((n, fields, 1, 8, lat), lambda g: (0, 0, g, 0, 0))

    adv = pl.pallas_call(
        functools.partial(advect_kernel, lon, tiles),
        grid=(groups,),
        out_shape=jax.ShapeDtypeStruct((fields, levels * lon, lat), f32),
        in_specs=[
            rows_spec(HALO),
            rows_spec(HALO),
            rows_spec(lon - 2 * HALO),
            rows_spec(HALO),
            rows_spec(HALO),
            packed_spec(lon),
            packed_spec(ext),
            pl.BlockSpec((1, 8, lat), lambda g: (g, 0, 0)),
            pl.BlockSpec(center.shape, lambda g: (0, 0)),
            pl.BlockSpec((1,) + edges.shape[1:], lambda g: (g, 0, 0, 0)),
            pl.BlockSpec((1,) + packed.shape[1:], lambda g: (g, 0, 0)),
            pl.BlockSpec((1,) + own_edges.shape[1:], lambda g: (g, 0, 0)),
        ],
        out_specs=pl.BlockSpec((fields, 8 * tiles * lon, lat), lambda g: (0, g, 0)),
        scratch_shapes=[
            pltpu.VMEM((4, fields, 8, lat), f32),
            pltpu.VMEM((ext * 48, 2 * lat), jnp.bfloat16),
            pltpu.VMEM(((ext - 4) * 48, 2 * lat), jnp.bfloat16),
            pltpu.VMEM(((ext - 4) * 48, 2 * lat), f32),
            pltpu.VMEM(((ext - 4) * 48, lat), f32),
        ],
        compiler_params=limit(36),
        cost_estimate=pl.CostEstimate(
            flops=60 * flat * lat, bytes_accessed=12 * flat * lat, transcendentals=0
        ),
        name="advect",
    )(left, lo, mid, hi, right, px, halo, inside, center, edges, packed, own_edges)
    return adv.reshape(state.shape), tend.reshape(state.shape)


def solution(mesh):
    in_specs = (P(None, None, "col", "row"), P("col", "row"), P("col", "row"), P(), P(), P())
    out_specs = (P(None, None, "col", "row"), P(None, None, "col", "row"))
    return jax.shard_map(local, mesh=mesh, in_specs=in_specs, out_specs=out_specs, check_vma=False)
```
